32 devices in a mesh: prompt: 2 (over core), sample: 4 (over y, x), head: 4 (over z).
Axes of the slice: x: 2, y: 2, z: 4, core: 2. Of those that a mesh axis runs over, the one named last changes fastest.
Arguments:
- queries: bfloat16 [8, 64, 4096], P('sample', None, 'head'), may hold values from -8 to 8
- prompt_keys: bfloat16 [4096, 512], P(('prompt', 'sample'), 'head'), may hold values from -3 to 3
- prompt_values: bfloat16 [4096, 512], P(('prompt', 'sample'), 'head'), may hold values from -4 to 4
- resp_keys: bfloat16 [8, 2048, 512], P('sample', 'prompt', 'head'), may hold values from -3 to 3
- resp_values: bfloat16 [8, 2048, 512], P('sample', 'prompt', 'head'), may hold values from -4 to 4
- cotangent: bfloat16 [8, 64, 4096], P('sample', None, 'head'), may hold values from -4 to 4
- lengths: int32 [8], replicated, may hold values from 1 to 2048, as said below
- offsets: int32 [8], replicated, may hold values from 0 to 2047, as said below
Outputs:
- attended: bfloat16 [8, 64, 4096], P('sample', None, 'head')
- grad_queries: bfloat16 [8, 64, 4096], P('sample', 'prompt', 'head')
- grad_prompt_keys: bfloat16 [4096, 512], P(('prompt', 'sample'), 'head')
- grad_prompt_values: bfloat16 [4096, 512], P(('prompt', 'sample'), 'head')
- grad_resp_keys: bfloat16 [8, 2048, 512], P('sample', 'prompt', 'head')
- grad_resp_values: bfloat16 [8, 2048, 512], P('sample', 'prompt', 'head')
The draws below stay inside these ranges and needn't reach their ends.
Inputs may be any that keep to these rules, and one draw needn't show every extreme that they name: `lengths`: some response has length 2048. `offsets`: each offset is below its response's length.
All inputs are finite; a program needn't handle non-finite values.
Results may differ from the reference program's by a relative error of at most 0.017.
Values may be sent and summed in bfloat16 or wider, within the bound.
A program may use at most 128 MiB of HBM per device.

```python
import math
from functools import partial
import jax
import jax.numpy as jnp
from jax import lax

HDIM = 128
GROUP = 8
WINDOW = 64
KV_HEADS = 4
QHEADS = 32
RESPONSES = 8
PROMPT = 4096
RESP_LEN = 2048


def response_bounds(key):
    key = jax.random.fold_in(key, 101)
    first, second, third = jax.random.split(key, 3)
    lengths = jax.random.randint(first, (RESPONSES,), 1, RESP_LEN + 1, dtype=jnp.int32)
    longest = jax.random.randint(second, (), 0, RESPONSES, dtype=jnp.int32)
    picked = jnp.arange(RESPONSES, dtype=jnp.int32) == longest
    lengths = jnp.where(picked, RESP_LEN, lengths).astype(jnp.int32)
    offsets = jax.random.randint(third, (RESPONSES,), 0, lengths, dtype=jnp.int32)
    offsets = jnp.where(picked, RESP_LEN - 1, offsets).astype(jnp.int32)
    return (lengths, offsets)


def draw_lengths(key, part):
    lengths, offsets = response_bounds(key)
    return lengths


def draw_offsets(key, part):
    lengths, offsets = response_bounds(key)
    return offsets


def draw_queries(key, part):
    key = jax.random.fold_in(key, 7)
    return jnp.clip(1.5 * jax.random.normal(key, (RESPONSES, WINDOW, QHEADS * HDIM), jnp.float32), -6.0, 6.0).astype(jnp.bfloat16)


def draw_prompt_keys(key, part):
    key = jax.random.fold_in(key, 8)
    return jnp.clip(jax.random.normal(key, (PROMPT, KV_HEADS * HDIM), jnp.float32), -3.0, 3.0).astype(jnp.bfloat16)


def shard_levels(own_key, shape, cuts, low, largest):
    def one(position, parts):
        draws = jax.random.uniform(jax.random.fold_in(jax.random.fold_in(own_key, 6), position), (parts,), jnp.float32, low / len(cuts), largest / len(cuts))
        return jnp.repeat(jnp.exp(draws), shape[position] // parts).reshape((-1,) + (1,) * (len(shape) - position - 1))

    level = one(*cuts[0])
    for cut in cuts[1:]:
        level = level * one(*cut)
    return level


def normal_values(key, shape, deviation, bound, pieces=(), kind=jnp.bfloat16):
    drawn = jax.random.normal(key, shape, jnp.float32) * deviation
    if len(pieces) > 0:
        drawn = shard_levels(key, shape, pieces, -0.22, 0.18) * drawn
    return jnp.clip(drawn, min=-bound, max=bound).astype(kind)


def setup_inputs(seed: int = 0) -> dict:
    key_list = jax.random.split(jax.random.key(seed), 9)
    queries = draw_queries(jax.random.fold_in(key_list[8], 71), 0)
    prompt_keys = draw_prompt_keys(jax.random.fold_in(key_list[8], 71), 0)
    prompt_values = normal_values(key_list[2], (PROMPT, KV_HEADS * HDIM), 1.0, 4.0, ((0, 8), (1, 4)))
    resp_keys = normal_values(key_list[3], (RESPONSES, RESP_LEN, KV_HEADS * HDIM), 1.0, 3.0, ((0, 4), (1, 2), (2, 4)))
    resp_values = normal_values(key_list[4], (RESPONSES, RESP_LEN, KV_HEADS * HDIM), 1.0, 4.0, ((0, 4), (1, 2), (2, 4)))
    cotangent = normal_values(key_list[5], (RESPONSES, WINDOW, QHEADS * HDIM), 1.0, 4.0, ((0, 4), (2, 4)))
    lengths = draw_lengths(jax.random.fold_in(key_list[8], 71), 0)
    offsets = draw_offsets(jax.random.fold_in(key_list[8], 71), 0)
    return {"queries": queries, "prompt_keys": prompt_keys, "prompt_values": prompt_values, "resp_keys": resp_keys, "resp_values": resp_values, "cotangent": cotangent, "lengths": lengths, "offsets": offsets}


NEG = -1e+30

def rounded(values):
    return lax.optimization_barrier(values.astype(jnp.bfloat16)).astype(jnp.float32)

def one_response(prompt_keys, prompt_values, carry, inputs):
    key_total, value_total = carry
    query, keys_own, values_own, grads, length, offset = inputs
    scale = 1.0 / math.sqrt(HDIM)
    line = jnp.arange(WINDOW, dtype=jnp.int32)
    places = jnp.arange(RESP_LEN, dtype=jnp.int32)
    keys = jnp.concatenate([prompt_keys, keys_own], axis=0).astype(jnp.float32)
    values = jnp.concatenate([prompt_values, values_own], axis=0).astype(jnp.float32)
    seen = jnp.concatenate([jnp.ones((WINDOW, PROMPT), jnp.bool_), places[None, :] <= offset + line[:, None]], axis=1)
    query_float = query.astype(jnp.float32)
    scores = jnp.einsum('cgd,kd->cgk', query_float, keys) * scale
    scores = jnp.where(seen[:, None, :], scores, NEG)
    top = lax.optimization_barrier(jnp.max(scores, axis=2))
    powers = jnp.exp(scores - top[..., None])
    total = lax.optimization_barrier(jnp.sum(powers, axis=2))
    output = jnp.einsum('cgk,kd->cgd', rounded(powers), values) / total[..., None]
    live = offset + line < length
    attended = jnp.where(live[:, None, None], output, 0.0).astype(jnp.bfloat16)
    log_total = top + jnp.log(total)
    grad_out = jnp.where(live[:, None, None], grads, jnp.zeros_like(grads))
    grad_float = grad_out.astype(jnp.float32)
    delta = lax.optimization_barrier(jnp.sum(grad_float * output, axis=2))
    probs = jnp.exp(scores - log_total[..., None])
    value_grad = jnp.einsum('cgk,cgd->kd', rounded(probs), grad_float)
    weight_grad = jnp.einsum('cgd,kd->cgk', grad_float, values)
    score_grad = rounded(probs * (weight_grad - delta[..., None]) * scale)
    query_grad = jnp.einsum('cgk,kd->cgd', score_grad, keys).astype(jnp.bfloat16)
    key_grad = jnp.einsum('cgk,cgd->kd', score_grad, query_float)
    carry = (key_total + key_grad[:PROMPT], value_total + value_grad[:PROMPT])
    return (carry, (attended, query_grad, key_grad[PROMPT:].astype(jnp.bfloat16), value_grad[PROMPT:].astype(jnp.bfloat16)))

def reference(queries, prompt_keys, prompt_values, resp_keys, resp_values, cotangent, lengths, offsets):
    query_heads = queries.reshape(RESPONSES, WINDOW, KV_HEADS, GROUP, HDIM).transpose(2, 0, 1, 3, 4)
    grad_heads = cotangent.reshape(RESPONSES, WINDOW, KV_HEADS, GROUP, HDIM).transpose(2, 0, 1, 3, 4)
    prompt_key_heads = prompt_keys.reshape(PROMPT, KV_HEADS, HDIM).transpose(1, 0, 2)
    prompt_value_heads = prompt_values.reshape(PROMPT, KV_HEADS, HDIM).transpose(1, 0, 2)
    resp_key_heads = resp_keys.reshape(RESPONSES, RESP_LEN, KV_HEADS, HDIM).transpose(2, 0, 1, 3)
    resp_value_heads = resp_values.reshape(RESPONSES, RESP_LEN, KV_HEADS, HDIM).transpose(2, 0, 1, 3)

    def per_head(inputs):
        query, grads, head_keys, head_values, own_keys, own_values = inputs
        start = (jnp.zeros((PROMPT, HDIM), jnp.float32), jnp.zeros((PROMPT, HDIM), jnp.float32))
        carry, results = lax.scan(partial(one_response, head_keys, head_values), start, (query, own_keys, own_values, grads, lengths, offsets))
        return results + (carry[0].astype(jnp.bfloat16), carry[1].astype(jnp.bfloat16))
    attended, query_grad, key_grad, value_grad, prompt_key_grad, prompt_value_grad = lax.map(per_head, (query_heads, grad_heads, prompt_key_heads, prompt_value_heads, resp_key_heads, resp_value_heads))
    attended = attended.transpose(1, 2, 0, 3, 4).reshape(RESPONSES, WINDOW, QHEADS * HDIM)
    query_grad = query_grad.transpose(1, 2, 0, 3, 4).reshape(RESPONSES, WINDOW, QHEADS * HDIM)
    key_grad = key_grad.transpose(1, 2, 0, 3).reshape(RESPONSES, RESP_LEN, KV_HEADS * HDIM)
    value_grad = value_grad.transpose(1, 2, 0, 3).reshape(RESPONSES, RESP_LEN, KV_HEADS * HDIM)
    prompt_key_grad = prompt_key_grad.transpose(1, 0, 2).reshape(PROMPT, KV_HEADS * HDIM)
    prompt_value_grad = prompt_value_grad.transpose(1, 0, 2).reshape(PROMPT, KV_HEADS * HDIM)
    return (attended, query_grad, prompt_key_grad, prompt_value_grad, key_grad, value_grad)
```

```python
import functools
import math

import jax
import jax.numpy as jnp
from jax import lax
from jax.experimental import pallas as pl
from jax.experimental.pallas import tpu as pltpu
from jax.sharding import PartitionSpec as P

NEG = -1e30
MESH = pl.DeviceIdType.MESH
F32 = jnp.float32
BF16 = jnp.bfloat16


def dot(a, b):
    return jnp.dot(a, b, preferred_element_type=F32)


def dot_nt(a, b):
    return lax.dot_general(a, b, (((1,), (1,)), ((), ())), preferred_element_type=F32)


def kernel(
    n_p,
    n_s,
    offsets,
    lengths,
    q_ref,
    pk_ref,
    pv_ref,
    rk_ref,
    rv_ref,
    g_ref,
    att_ref,
    gq_ref,
    gpk_ref,
    gpv_ref,
    grk_ref,
    grv_ref,
    kv,
    qrows,
    grows,
    g_t,
    p_all,
    p_own,
    ds,
    g_scaled,
    small_t,
    acc,
    acc_in,
    out_t,
    tops,
    stats,
    gq_t,
    kvg_own,
    kvg_out,
    kvg_in,
    gq_out,
    gq_in,
    kv_send,
    kv_recv,
    acc_send,
    acc_recv,
    kvg_send,
    kvg_recv,
    gq_send,
    gq_recv,
):
    count, window, wide = q_ref.shape
    width, depth = pk_ref.shape
    span = rk_ref.shape[1]
    group = wide // depth
    height = window * group
    rows = count * height
    tile = math.gcd(height, 256)
    per = height // tile
    scale = 1.0 / math.sqrt(depth)
    c = scale * math.log2(math.e)
    me_s = lax.axis_index("sample")
    me_p = lax.axis_index("prompt")
    part = window // n_p

    def to_sample(k):
        if n_s == 4:
            return ((me_s // 2 + k // 2) % 2) * 2 + (me_s % 2 + k % 2) % 2
        return (me_s + k) % n_s

    def from_sample(k):
        if n_s == 4:
            return to_sample(k)
        return (me_s + n_s - k) % n_s

    barrier = pltpu.get_barrier_semaphore()
    for k in range(1, n_s):
        pl.semaphore_signal(barrier, inc=1, device_id={"sample": to_sample(k)}, device_id_type=MESH)
    for k in range(1, n_p):
        pl.semaphore_signal(
            barrier, inc=1, device_id={"prompt": (me_p + k) % n_p}, device_id_type=MESH
        )
    pl.semaphore_wait(barrier, n_s - 1 + n_p - 1)

    kv_copies = {}
    for k in range(1, n_s):
        for j, ref in enumerate((pk_ref, pv_ref)):
            copy = pltpu.make_async_remote_copy(
                src_ref=ref,
                dst_ref=kv.at[k - 1, j],
                send_sem=kv_send.at[k - 1, j],
                recv_sem=kv_recv.at[k - 1, j],
                device_id={"sample": to_sample(k)},
                device_id_type=MESH,
            )
            copy.start()
            kv_copies[k, j] = copy

    own = [(offsets[me_s * count + r], lengths[me_s * count + r]) for r in range(count)]
    line = lax.broadcasted_iota(jnp.int32, (window, 1), 0)
    for r in range(count):
        live = own[r][0] + line < own[r][1]
        for h in range(group):
            at = pl.ds(r * height + h * window, window)
            head = pl.ds(h * depth, depth)
            qrows[at, :] = q_ref[r, :, head]
            grows[at, :] = jnp.where(live, g_ref[r, :, head].astype(F32), 0.0).astype(BF16)
    for i in range(rows // tile):
        at = pl.ds(i * tile, tile)
        g_t[:, at] = grows[at, :].T

    def forward(seg, keys, values, p_ref, low, high, mask, first):
        size = keys.shape[0]
        small_t[:, :size] = values[...].T

        def visit(i, _):
            at = pl.ds(pl.multiple_of(i * tile, tile), tile)
            scores = dot_nt(keys[...], qrows[at, :])
            if mask is not None:
                scores = mask(scores)
            top = jnp.max(scores, axis=0, keepdims=True)
            powers = jnp.exp2((scores - top) * c)
            total = jnp.sum(powers, axis=0, keepdims=True)
            low_powers = powers.astype(BF16)
            p_ref[:, at] = low_powers
            weighted = dot(small_t[:, :size], low_powers)
            tops[seg : seg + 1, at] = top
            if first:
                acc[0:depth, at] = weighted
                acc[depth : depth + 1, at] = top
                acc[depth + 1 : depth + 2, at] = total
            else:
                before = acc[depth : depth + 1, at]
                fresh = jnp.maximum(before, top)
                old = jnp.exp2((before - fresh) * c)
                new = jnp.exp2((top - fresh) * c)
                acc[0:depth, at] = acc[0:depth, at] * old + weighted * new
                acc[depth : depth + 1, at] = fresh
                acc[depth + 1 : depth + 2, at] = acc[depth + 1 : depth + 2, at] * old + total * new
            return 0

        lax.fori_loop(low, high, visit, 0)

    for r in range(count):
        key_place = me_p * span + lax.broadcasted_iota(jnp.int32, (span, 1), 0)
        row_place = own[r][0] + lax.broadcasted_iota(jnp.int32, (1, tile), 1) % window

        def mask(scores):
            return jnp.where(key_place <= row_place, scores, NEG)

        forward(n_s, rk_ref.at[r], rv_ref.at[r], p_own, r * per, (r + 1) * per, mask, True)
    forward(0, pk_ref, pv_ref, p_all.at[0], 0, count * per, None, False)
    for k in range(1, n_s):
        kv_copies[k, 0].wait_recv()
        kv_copies[k, 1].wait_recv()
        forward(
            k, kv.at[k - 1, 0], kv.at[k - 1, 1], p_all.at[k], 0, count * per, None, False
        )

    acc_copies = []
    for k in range(1, n_p):
        copy = pltpu.make_async_remote_copy(
            src_ref=acc,
            dst_ref=acc_in.at[k - 1],
            send_sem=acc_send.at[k - 1],
            recv_sem=acc_recv.at[k - 1],
            device_id={"prompt": (me_p + k) % n_p},
            device_id_type=MESH,
        )
        copy.start()
        acc_copies.append(copy)
    for copy in acc_copies:
        copy.wait_recv()

    for i in range(rows // tile):
        at = pl.ds(i * tile, tile)
        top = acc[depth : depth + 1, at]
        for k in range(n_p - 1):
            top = jnp.maximum(top, acc_in[k, depth : depth + 1, at])
        decay = jnp.exp2((acc[depth : depth + 1, at] - top) * c)
        total = acc[depth + 1 : depth + 2, at] * decay
        weighted = acc[0:depth, at] * decay
        for k in range(n_p - 1):
            decay = jnp.exp2((acc_in[k, depth : depth + 1, at] - top) * c)
            total = total + acc_in[k, depth + 1 : depth + 2, at] * decay
            weighted = weighted + acc_in[k, 0:depth, at] * decay
        inverse = 1.0 / total
        output = weighted * inverse
        out_t[:, at] = output
        stats[0:1, at] = top
        stats[1:2, at] = inverse
        gq_t[:, at] = jnp.zeros((depth, tile), F32)
        r = i // per
        live = own[r][0] + line < own[r][1]
        by_row = output.T
        for part_h in range(tile // window):
            h = (i % per) * (tile // window) + part_h
            block = by_row[part_h * window : (part_h + 1) * window]
            att_ref[r, :, pl.ds(h * depth, depth)] = jnp.where(live, block, 0.0).astype(BF16)

    def backward(seg, keys, values, p_ref, low, high):
        size = keys.shape[0]
        small_t[:, :size] = keys[...].T

        def visit(i, _):
            at = pl.ds(pl.multiple_of(i * tile, tile), tile)
            factor = jnp.exp2((tops[seg : seg + 1, at] - stats[0:1, at]) * c) * stats[1:2, at]
            grads = (g_t[:, at].astype(F32) * factor).astype(BF16)
            delta = jnp.sum(grads.astype(F32) * out_t[:, at], axis=0, keepdims=True)
            g_scaled[at, :] = grads.T
            weight_grad = dot(values[...], grads)
            score_grad = (p_ref[:, at].astype(F32) * (weight_grad - delta)).astype(BF16)
            ds[:size, at] = score_grad
            gq_t[:, at] += dot(small_t[:, :size], score_grad)
            return 0

        lax.fori_loop(low, high, visit, 0)
        span_rows = slice(low * tile, high * tile)
        value_grad = dot(p_ref[:, span_rows], g_scaled[span_rows, :])
        key_grad = dot(ds[:size, span_rows], qrows[span_rows, :]) * scale
        return key_grad, value_grad

    kvg_copies = []
    for k in range(n_s - 1, 0, -1):
        key_grad, value_grad = backward(
            k, kv.at[k - 1, 0], kv.at[k - 1, 1], p_all.at[k], 0, count * per
        )
        kvg_out[k - 1, 0] = key_grad.astype(BF16)
        kvg_out[k - 1, 1] = value_grad.astype(BF16)
        copy = pltpu.make_async_remote_copy(
            src_ref=kvg_out.at[k - 1],
            dst_ref=kvg_in.at[k - 1],
            send_sem=kvg_send.at[k - 1],
            recv_sem=kvg_recv.at[k - 1],
            device_id={"sample": from_sample(k)},
            device_id_type=MESH,
        )
        copy.start()
        kvg_copies.append(copy)
    key_grad, value_grad = backward(0, pk_ref, pv_ref, p_all.at[0], 0, count * per)
    kvg_own[0] = key_grad
    kvg_own[1] = value_grad
    for r in range(count):
        key_grad, value_grad = backward(
            n_s, rk_ref.at[r], rv_ref.at[r], p_own, r * per, (r + 1) * per
        )
        grk_ref[r] = key_grad.astype(BF16)
        grv_ref[r] = value_grad.astype(BF16)

    for i in range(rows // tile):
        at = pl.ds(i * tile, tile)
        r = i // per
        by_row = gq_t[:, at].T * scale
        for part_h in range(tile // window):
            h = (i % per) * (tile // window) + part_h
            for to in range(n_p):
                first = part_h * window + to * part
                gq_out[to, r, :, pl.ds(h * depth, depth)] = by_row[first : first + part]
    gq_copies = []
    for k in range(1, n_p):
        to = (me_p + k) % n_p
        copy = pltpu.make_async_remote_copy(
            src_ref=gq_out.at[to],
            dst_ref=gq_in.at[k - 1],
            send_sem=gq_send.at[k - 1],
            recv_sem=gq_recv.at[k - 1],
            device_id={"prompt": to},
            device_id_type=MESH,
        )
        copy.start()
        gq_copies.append(copy)
    for copy in kvg_copies:
        copy.wait_recv()
    for j, ref in enumerate((gpk_ref, gpv_ref)):
        total = kvg_own[j]
        for k in range(n_s - 1):
            total = total + kvg_in[k, j].astype(F32)
        ref[...] = total.astype(BF16)
    for copy in gq_copies:
        copy.wait_recv()
    total = gq_out[me_p]
    for k in range(n_p - 1):
        total = total + gq_in[k]
    gq_ref[...] = total.astype(BF16)

    for copy in kv_copies.values():
        copy.wait_send()
    for copy in acc_copies + kvg_copies + gq_copies:
        copy.wait_send()


def local(n_p, n_s, queries, prompt_keys, prompt_values, resp_keys, resp_values, cotangent, lengths, offsets):
    count, window, wide = queries.shape
    width, depth = prompt_keys.shape
    span = resp_keys.shape[1]
    rows = count * window * (wide // depth)
    tall = depth + 8
    vmem = pl.BlockSpec(memory_space=pltpu.VMEM)
    smem = pl.BlockSpec(memory_space=pltpu.SMEM)
    shape = jax.ShapeDtypeStruct
    dma = pltpu.SemaphoreType.DMA
    peers = max(n_p - 1, 1)
    others = max(n_s - 1, 1)
    scratch = [
        pltpu.VMEM((others, 2, width, depth), BF16),
        pltpu.VMEM((rows, depth), BF16),
        pltpu.VMEM((rows, depth), BF16),
        pltpu.VMEM((depth, rows), BF16),
        pltpu.VMEM((n_s, width, rows), BF16),
        pltpu.VMEM((span, rows), BF16),
        pltpu.VMEM((max(span, width), rows), BF16),
        pltpu.VMEM((rows, depth), BF16),
        pltpu.VMEM((depth, max(span, width)), BF16),
        pltpu.VMEM((tall, rows), F32),
        pltpu.VMEM((peers, tall, rows), F32),
        pltpu.VMEM((depth, rows), F32),
        pltpu.VMEM((-(-(n_s + 1) // 8) * 8, rows), F32),
        pltpu.VMEM((8, rows), F32),
        pltpu.VMEM((depth, rows), F32),
        pltpu.VMEM((2, width, depth), F32),
        pltpu.VMEM((others, 2, width, depth), BF16),
        pltpu.VMEM((others, 2, width, depth), BF16),
        pltpu.VMEM((n_p, count, window // n_p, wide), F32),
        pltpu.VMEM((peers, count, window // n_p, wide), F32),
        dma((others, 2)),
        dma((others, 2)),
        dma((peers,)),
        dma((peers,)),
        dma((others,)),
        dma((others,)),
        dma((peers,)),
        dma((peers,)),
    ]
    return pl.pallas_call(
        functools.partial(kernel, n_p, n_s),
        out_shape=(
            shape(queries.shape, BF16),
            shape((count, window // n_p, wide), BF16),
            shape(prompt_keys.shape, BF16),
            shape(prompt_values.shape, BF16),
            shape(resp_keys.shape, BF16),
            shape(resp_values.shape, BF16),
        ),
        in_specs=[smem] * 2 + [vmem] * 6,
        out_specs=[vmem] * 6,
        scratch_shapes=scratch,
        compiler_params=pltpu.CompilerParams(
            collective_id=0, has_side_effects=True, vmem_limit_bytes=52 * 1024 * 1024
        ),
    )(offsets, lengths, queries, prompt_keys, prompt_values, resp_keys, resp_values, cotangent)


def solution(mesh):
    return jax.shard_map(
        functools.partial(local, mesh.shape["prompt"], mesh.shape["sample"]),
        mesh=mesh,
        in_specs=(
            P("sample", None, "head"),
            P(("prompt", "sample"), "head"),
            P(("prompt", "sample"), "head"),
            P("sample", "prompt", "head"),
            P("sample", "prompt", "head"),
            P("sample", None, "head"),
            P(),
            P(),
        ),
        out_specs=(
            P("sample", None, "head"),
            P("sample", "prompt", "head"),
            P(("prompt", "sample"), "head"),
            P(("prompt", "sample"), "head"),
            P("sample", "prompt", "head"),
            P("sample", "prompt", "head"),
        ),
        check_vma=False,
    )
```

```python
import functools
import math

import jax
import jax.numpy as jnp
from jax import lax
from jax.experimental import pallas as pl
from jax.experimental.pallas import tpu as pltpu
from jax.sharding import PartitionSpec as P

NEG = -1e30
MESH = pl.DeviceIdType.MESH
F32 = jnp.float32
BF16 = jnp.bfloat16


def dot(a, b):
    return jnp.dot(a, b, preferred_element_type=F32)


def dot_nt(a, b):
    return lax.dot_general(a, b, (((1,), (1,)), ((), ())), preferred_element_type=F32)


def kernel(
    n_p,
    n_s,
    offsets_hbm,
    lengths_hbm,
    q_hbm,
    pk_hbm,
    pv_hbm,
    rk_hbm,
    rv_hbm,
    g_hbm,
    att_ref,
    gq_ref,
    gpk_ref,
    gpv_ref,
    grk_ref,
    grv_ref,
    offsets,
    lengths,
    q_ref,
    pk_ref,
    pv_ref,
    rk_ref,
    rv_ref,
    g_ref,
    kv,
    qrows,
    grows,
    g_t,
    p_all,
    p_own,
    ds,
    g_scaled,
    small_t,
    acc,
    acc_in,
    out_t,
    tops,
    stats,
    gq_t,
    kvg_own,
    kvg_out,
    kvg_in,
    gq_out,
    gq_in,
    kv_send,
    kv_recv,
    acc_send,
    acc_recv,
    kvg_send,
    kvg_recv,
    gq_send,
    gq_recv,
    load_sem,
):
    count, window, wide = q_ref.shape
    width, depth = pk_ref.shape
    span = rk_ref.shape[1]
    group = wide // depth
    height = window * group
    rows = count * height
    tile = math.gcd(height, 256)
    per = height // tile
    scale = 1.0 / math.sqrt(depth)
    c = scale * math.log2(math.e)
    me_s = lax.axis_index("sample")
    me_p = lax.axis_index("prompt")
    part = window // n_p

    def to_sample(k):
        if n_s == 4:
            return ((me_s // 2 + k // 2) % 2) * 2 + (me_s % 2 + k % 2) % 2
        return (me_s + k) % n_s

    def from_sample(k):
        if n_s == 4:
            return to_sample(k)
        return (me_s + n_s - k) % n_s

    loads = {}
    for name, src, dst in (
        ("offsets", offsets_hbm, offsets),
        ("lengths", lengths_hbm, lengths),
        ("q", q_hbm, q_ref),
        ("rk", rk_hbm, rk_ref),
        ("rv", rv_hbm, rv_ref),
        ("pk", pk_hbm, pk_ref),
        ("pv", pv_hbm, pv_ref),
        ("g", g_hbm, g_ref),
    ):
        loads[name] = pltpu.make_async_copy(src, dst, load_sem.at[len(loads)])
        loads[name].start()

    barrier = pltpu.get_barrier_semaphore()
    for k in range(1, n_s):
        pl.semaphore_signal(barrier, inc=1, device_id={"sample": to_sample(k)}, device_id_type=MESH)
    for k in range(1, n_p):
        pl.semaphore_signal(
            barrier, inc=1, device_id={"prompt": (me_p + k) % n_p}, device_id_type=MESH
        )
    pl.semaphore_wait(barrier, n_s - 1 + n_p - 1)

    kv_copies = {}

    def send_kv(k, j, src, to):
        copy = pltpu.make_async_remote_copy(
            src_ref=src,
            dst_ref=kv.at[k - 1, j],
            send_sem=kv_send.at[k - 1, j],
            recv_sem=kv_recv.at[k - 1, j],
            device_id={"sample": to_sample(to)},
            device_id_type=MESH,
        )
        copy.start()
        kv_copies[k, j] = copy

    relay = n_s == 4
    mine = (pk_hbm, pv_hbm)
    if relay:
        for k, j in ((1, 0), (2, 1), (1, 1), (2, 0)):
            send_kv(k, j, mine[j], k)
    else:
        for k in range(1, n_s):
            for j in range(2):
                send_kv(k, j, mine[j], k)

    def forward(seg, keys, values, p_ref, low, high, mask, first):
        size = keys.shape[0]
        small_t[:, :size] = values[...].T

        def visit(i, _):
            at = pl.ds(pl.multiple_of(i * tile, tile), tile)
            scores = dot_nt(keys[...], qrows[at, :])
            if mask is not None:
                scores = mask(scores)
            top = jnp.max(scores, axis=0, keepdims=True)
            powers = jnp.exp2((scores - top) * c)
            total = jnp.sum(powers, axis=0, keepdims=True)
            low_powers = powers.astype(BF16)
            p_ref[:, at] = low_powers
            weighted = dot(small_t[:, :size], low_powers)
            tops[seg : seg + 1, at] = top
            if first:
                acc[0:depth, at] = weighted
                acc[depth : depth + 1, at] = top
                acc[depth + 1 : depth + 2, at] = total
            else:
                before = acc[depth : depth + 1, at]
                fresh = jnp.maximum(before, top)
                old = jnp.exp2((before - fresh) * c)
                new = jnp.exp2((top - fresh) * c)
                acc[0:depth, at] = acc[0:depth, at] * old + weighted * new
                acc[depth : depth + 1, at] = fresh
                acc[depth + 1 : depth + 2, at] = acc[depth + 1 : depth + 2, at] * old + total * new
            return 0

        lax.fori_loop(low, high, visit, 0, unroll=True)

    def own_forward():
        for r in range(count):
            key_place = me_p * span + lax.broadcasted_iota(jnp.int32, (span, 1), 0)
            row_place = own[r][0] + lax.broadcasted_iota(jnp.int32, (1, tile), 1) % window

            def mask(scores):
                return jnp.where(key_place <= row_place, scores, NEG)

            forward(n_s, rk_ref.at[r], rv_ref.at[r], p_own, r * per, (r + 1) * per, mask, True)

    for name in ("offsets", "lengths", "q"):
        loads[name].wait()
    own = [(offsets[me_s * count + r], lengths[me_s * count + r]) for r in range(count)]
    line = lax.broadcasted_iota(jnp.int32, (window, 1), 0)
    for r in range(count):
        for h in range(group):
            at = pl.ds(r * height + h * window, window)
            head = pl.ds(h * depth, depth)
            qrows[at, :] = q_ref[r, :, head]
    loads["rk"].wait()
    loads["rv"].wait()
    own_forward()
    if relay:
        kv_copies[1, 0].wait_recv()
        send_kv(3, 0, kv.at[0, 0], 2)
        kv_copies[2, 1].wait_recv()
        send_kv(3, 1, kv.at[1, 1], 1)
    loads["g"].wait()
    for r in range(count):
        live = own[r][0] + line < own[r][1]
        for h in range(group):
            at = pl.ds(r * height + h * window, window)
            head = pl.ds(h * depth, depth)
            grows[at, :] = jnp.where(live, g_ref[r, :, head].astype(F32), 0.0).astype(BF16)
    for i in range(rows // tile):
        at = pl.ds(i * tile, tile)
        g_t[:, at] = grows[at, :].T

    loads["pk"].wait()
    loads["pv"].wait()
    forward(0, pk_ref, pv_ref, p_all.at[0], 0, count * per, None, False)
    acc_copies = []
    for k in range(1, n_s):
        for j in range(2):
            if not relay or (k, j) not in ((1, 0), (2, 1)):
                kv_copies[k, j].wait_recv()
        halves = count if k == n_s - 1 else 1
        for half in range(halves):
            low, high = half * count * per // halves, (half + 1) * count * per // halves
            forward(k, kv.at[k - 1, 0], kv.at[k - 1, 1], p_all.at[k], low, high, None, False)
            if k < n_s - 1:
                continue
            at = pl.ds(low * tile, (high - low) * tile)
            for to in range(1, n_p):
                copy = pltpu.make_async_remote_copy(
                    src_ref=acc.at[:, at],
                    dst_ref=acc_in.at[to - 1, :, at],
                    send_sem=acc_send.at[to - 1, half],
                    recv_sem=acc_recv.at[to - 1, half],
                    device_id={"prompt": (me_p + to) % n_p},
                    device_id_type=MESH,
                )
                copy.start()
                acc_copies.append((half, copy))

    for i in range(rows // tile):
        if i % per == 0:
            for half, copy in acc_copies:
                if half == i // per:
                    copy.wait_recv()
        at = pl.ds(i * tile, tile)
        top = acc[depth : depth + 1, at]
        for k in range(n_p - 1):
            top = jnp.maximum(top, acc_in[k, depth : depth + 1, at])
        decay = jnp.exp2((acc[depth : depth + 1, at] - top) * c)
        total = acc[depth + 1 : depth + 2, at] * decay
        weighted = acc[0:depth, at] * decay
        for k in range(n_p - 1):
            decay = jnp.exp2((acc_in[k, depth : depth + 1, at] - top) * c)
            total = total + acc_in[k, depth + 1 : depth + 2, at] * decay
            weighted = weighted + acc_in[k, 0:depth, at] * decay
        inverse = 1.0 / total
        output = weighted * inverse
        out_t[:, at] = output
        stats[0:1, at] = top
        stats[1:2, at] = inverse
        gq_t[:, at] = jnp.zeros((depth, tile), F32)
        r = i // per
        live = own[r][0] + line < own[r][1]
        by_row = output.T
        for part_h in range(tile // window):
            h = (i % per) * (tile // window) + part_h
            block = by_row[part_h * window : (part_h + 1) * window]
            att_ref[r, :, pl.ds(h * depth, depth)] = jnp.where(live, block, 0.0).astype(BF16)

    def backward(seg, keys, values, p_ref, low, high):
        size = keys.shape[0]
        small_t[:, :size] = keys[...].T

        def visit(i, _):
            at = pl.ds(pl.multiple_of(i * tile, tile), tile)
            factor = jnp.exp2((tops[seg : seg + 1, at] - stats[0:1, at]) * c) * stats[1:2, at]
            grads = (g_t[:, at].astype(F32) * factor).astype(BF16)
            delta = jnp.sum(grads.astype(F32) * out_t[:, at], axis=0, keepdims=True)
            g_scaled[at, :] = grads.T
            weight_grad = dot(values[...], grads)
            score_grad = p_ref[:, at] * (weight_grad - delta).astype(BF16)
            ds[:size, at] = score_grad
            gq_t[:, at] += dot(small_t[:, :size], score_grad)
            return 0

        lax.fori_loop(low, high, visit, 0, unroll=True)
        span_rows = slice(low * tile, high * tile)
        value_grad = dot(p_ref[:, span_rows], g_scaled[span_rows, :])
        key_grad = dot(ds[:size, span_rows], qrows[span_rows, :]) * scale
        return key_grad, value_grad

    kvg_copies = []
    for k in range(n_s - 1, 0, -1):
        key_grad, value_grad = backward(
            k, kv.at[k - 1, 0], kv.at[k - 1, 1], p_all.at[k], 0, count * per
        )
        kvg_out[k - 1, 0] = key_grad.astype(BF16)
        kvg_out[k - 1, 1] = value_grad.astype(BF16)
        copy = pltpu.make_async_remote_copy(
            src_ref=kvg_out.at[k - 1],
            dst_ref=kvg_in.at[k - 1],
            send_sem=kvg_send.at[k - 1],
            recv_sem=kvg_recv.at[k - 1],
            device_id={"sample": from_sample(k)},
            device_id_type=MESH,
        )
        copy.start()
        kvg_copies.append(copy)
    key_grad, value_grad = backward(0, pk_ref, pv_ref, p_all.at[0], 0, count * per)
    kvg_own[0] = key_grad
    kvg_own[1] = value_grad
    for r in range(count):
        key_grad, value_grad = backward(
            n_s, rk_ref.at[r], rv_ref.at[r], p_own, r * per, (r + 1) * per
        )
        grk_ref[r] = key_grad.astype(BF16)
        grv_ref[r] = value_grad.astype(BF16)

    for i in range(rows // tile):
        at = pl.ds(i * tile, tile)
        r = i // per
        by_row = gq_t[:, at].T * scale
        for part_h in range(tile // window):
            h = (i % per) * (tile // window) + part_h
            for to in range(n_p):
                first = part_h * window + to * part
                gq_out[to, r, :, pl.ds(h * depth, depth)] = by_row[first : first + part]
    gq_copies = []
    for k in range(1, n_p):
        to = (me_p + k) % n_p
        copy = pltpu.make_async_remote_copy(
            src_ref=gq_out.at[to],
            dst_ref=gq_in.at[k - 1],
            send_sem=gq_send.at[k - 1],
            recv_sem=gq_recv.at[k - 1],
            device_id={"prompt": to},
            device_id_type=MESH,
        )
        copy.start()
        gq_copies.append(copy)
    for copy in kvg_copies:
        copy.wait_recv()
    for j, ref in enumerate((gpk_ref, gpv_ref)):
        total = kvg_own[j]
        for k in range(n_s - 1):
            total = total + kvg_in[k, j].astype(F32)
        ref[...] = total.astype(BF16)
    for copy in gq_copies:
        copy.wait_recv()
    total = gq_out[me_p]
    for k in range(n_p - 1):
        total = total + gq_in[k]
    gq_ref[...] = total.astype(BF16)

    for copy in kv_copies.values():
        copy.wait_send()
    for copy in [copy for _, copy in acc_copies] + kvg_copies + gq_copies:
        copy.wait_send()


def write_out(*refs):
    sem = refs[-1]
    half = len(refs) // 2
    copies = [
        pltpu.make_async_copy(refs[i], refs[half + i], sem.at[i]) for i in range(half)
    ]
    for copy in copies:
        copy.start()
    for copy in copies:
        copy.wait()


def local(n_p, n_s, queries, prompt_keys, prompt_values, resp_keys, resp_values, cotangent, lengths, offsets):
    count, window, wide = queries.shape
    width, depth = prompt_keys.shape
    span = resp_keys.shape[1]
    rows = count * window * (wide // depth)
    tall = depth + 8
    vmem = pl.BlockSpec(memory_space=pltpu.VMEM)
    hbm = pl.BlockSpec(memory_space=pltpu.HBM)
    shape = jax.ShapeDtypeStruct
    dma = pltpu.SemaphoreType.DMA
    peers = max(n_p - 1, 1)
    others = max(n_s - 1, 1)
    scratch = [
        pltpu.SMEM(offsets.shape, offsets.dtype),
        pltpu.SMEM(lengths.shape, lengths.dtype),
        pltpu.VMEM(queries.shape, BF16),
        pltpu.VMEM(prompt_keys.shape, BF16),
        pltpu.VMEM(prompt_values.shape, BF16),
        pltpu.VMEM(resp_keys.shape, BF16),
        pltpu.VMEM(resp_values.shape, BF16),
        pltpu.VMEM(cotangent.shape, BF16),
        pltpu.VMEM((others, 2, width, depth), BF16),
        pltpu.VMEM((rows, depth), BF16),
        pltpu.VMEM((rows, depth), BF16),
        pltpu.VMEM((depth, rows), BF16),
        pltpu.VMEM((n_s, width, rows), BF16),
        pltpu.VMEM((span, rows), BF16),
        pltpu.VMEM((max(span, width), rows), BF16),
        pltpu.VMEM((rows, depth), BF16),
        pltpu.VMEM((depth, max(span, width)), BF16),
        pltpu.VMEM((tall, rows), F32),
        pltpu.VMEM((peers, tall, rows), F32),
        pltpu.VMEM((depth, rows), F32),
        pltpu.VMEM((-(-(n_s + 1) // 8) * 8, rows), F32),
        pltpu.VMEM((8, rows), F32),
        pltpu.VMEM((depth, rows), F32),
        pltpu.VMEM((2, width, depth), F32),
        pltpu.VMEM((others, 2, width, depth), BF16),
        pltpu.VMEM((others, 2, width, depth), BF16),
        pltpu.VMEM((n_p, count, window // n_p, wide), F32),
        pltpu.VMEM((peers, count, window // n_p, wide), F32),
        dma((others, 2)),
        dma((others, 2)),
        dma((peers, count)),
        dma((peers, count)),
        dma((others,)),
        dma((others,)),
        dma((peers,)),
        dma((peers,)),
        dma((8,)),
    ]
    results = pl.pallas_call(
        functools.partial(kernel, n_p, n_s),
        out_shape=(
            shape(queries.shape, BF16),
            shape((count, window // n_p, wide), BF16),
            shape(prompt_keys.shape, BF16),
            shape(prompt_values.shape, BF16),
            shape(resp_keys.shape, BF16),
            shape(resp_values.shape, BF16),
        ),
        in_specs=[hbm] * 8,
        out_specs=[vmem] * 6,
        scratch_shapes=scratch,
        compiler_params=pltpu.CompilerParams(
            collective_id=0, has_side_effects=True, vmem_limit_bytes=62 * 1024 * 1024
        ),
    )(offsets, lengths, queries, prompt_keys, prompt_values, resp_keys, resp_values, cotangent)
    return pl.pallas_call(
        write_out,
        out_shape=tuple(shape(result.shape, result.dtype) for result in results),
        in_specs=[vmem] * len(results),
        out_specs=[hbm] * len(results),
        scratch_shapes=[dma((len(results),))],
        compiler_params=pltpu.CompilerParams(vmem_limit_bytes=4 * 1024 * 1024),
    )(*results)


def solution(mesh):
    return jax.shard_map(
        functools.partial(local, mesh.shape["prompt"], mesh.shape["sample"]),
        mesh=mesh,
        in_specs=(
            P("sample", None, "head"),
            P(("prompt", "sample"), "head"),
            P(("prompt", "sample"), "head"),
            P("sample", "prompt", "head"),
            P("sample", "prompt", "head"),
            P("sample", None, "head"),
            P(),
            P(),
        ),
        out_specs=(
            P("sample", None, "head"),
            P("sample", "prompt", "head"),
            P(("prompt", "sample"), "head"),
            P(("prompt", "sample"), "head"),
            P("sample", "prompt", "head"),
            P("sample", "prompt", "head"),
        ),
        check_vma=False,
    )
```

```python
import functools
import math

import jax
import jax.numpy as jnp
from jax import lax
from jax.experimental import pallas as pl
from jax.experimental.pallas import tpu as pltpu
from jax.sharding import PartitionSpec as P

NEG = -1e30
MESH = pl.DeviceIdType.MESH
F32 = jnp.float32
BF16 = jnp.bfloat16


def dot(a, b):
    return jnp.dot(a, b, preferred_element_type=F32)


def dot_nt(a, b):
    return lax.dot_general(a, b, (((1,), (1,)), ((), ())), preferred_element_type=F32)


def kernel(
    n_p,
    n_s,
    offsets_hbm,
    lengths_hbm,
    q_hbm,
    pk_hbm,
    pv_hbm,
    rk_hbm,
    rv_hbm,
    g_hbm,
    att_hbm,
    gq_hbm,
    gpk_hbm,
    gpv_hbm,
    grk_hbm,
    grv_hbm,
    att_ref,
    gq_ref,
    gpk_ref,
    gpv_ref,
    grk_ref,
    grv_ref,
    offsets,
    lengths,
    q_ref,
    pk_ref,
    pv_ref,
    rk_ref,
    rv_ref,
    g_ref,
    kv,
    qrows,
    grows,
    g_t,
    p_all,
    p_own,
    ds,
    g_scaled,
    small_t,
    acc,
    acc_in,
    out_t,
    tops,
    stats,
    gq_t,
    kvg_own,
    kvg_out,
    kvg_in,
    gq_out,
    gq_in,
    kv_send,
    kv_recv,
    acc_send,
    acc_recv,
    kvg_send,
    kvg_recv,
    gq_send,
    gq_recv,
    load_sem,
    store_sem,
):
    count, window, wide = q_ref.shape
    width, depth = pk_ref.shape
    span = rk_ref.shape[1]
    group = wide // depth
    height = window * group
    rows = count * height
    tile = math.gcd(height, 256)
    per = height // tile
    scale = 1.0 / math.sqrt(depth)
    c = scale * math.log2(math.e)
    me_s = lax.axis_index("sample")
    me_p = lax.axis_index("prompt")
    part = window // n_p

    def to_sample(k):
        if n_s == 4:
            return ((me_s // 2 + k // 2) % 2) * 2 + (me_s % 2 + k % 2) % 2
        return (me_s + k) % n_s

    def from_sample(k):
        if n_s == 4:
            return to_sample(k)
        return (me_s + n_s - k) % n_s

    loads = {}
    for name, src, dst in (
        ("offsets", offsets_hbm, offsets),
        ("lengths", lengths_hbm, lengths),
        ("q", q_hbm, q_ref),
        ("rk", rk_hbm, rk_ref),
        ("rv", rv_hbm, rv_ref),
        ("pk", pk_hbm, pk_ref),
        ("pv", pv_hbm, pv_ref),
        ("g", g_hbm, g_ref),
    ):
        loads[name] = pltpu.make_async_copy(src, dst, load_sem.at[len(loads)])
        loads[name].start()

    barrier = pltpu.get_barrier_semaphore()
    for k in range(1, n_s):
        pl.semaphore_signal(barrier, inc=1, device_id={"sample": to_sample(k)}, device_id_type=MESH)
    for k in range(1, n_p):
        pl.semaphore_signal(
            barrier, inc=1, device_id={"prompt": (me_p + k) % n_p}, device_id_type=MESH
        )
    pl.semaphore_wait(barrier, n_s - 1 + n_p - 1)

    stores = []

    def store(src, dst):
        stores.append(pltpu.make_async_copy(src, dst, store_sem.at[len(stores)]))
        stores[-1].start()

    kv_copies = {}

    def send_kv(k, j, src, to):
        copy = pltpu.make_async_remote_copy(
            src_ref=src,
            dst_ref=kv.at[k - 1, j],
            send_sem=kv_send.at[k - 1, j],
            recv_sem=kv_recv.at[k - 1, j],
            device_id={"sample": to_sample(to)},
            device_id_type=MESH,
        )
        copy.start()
        kv_copies[k, j] = copy

    relay = n_s == 4
    mine = (pk_hbm, pv_hbm)
    if relay:
        for k, j in ((1, 0), (2, 1), (1, 1), (2, 0)):
            send_kv(k, j, mine[j], k)
    else:
        for k in range(1, n_s):
            for j in range(2):
                send_kv(k, j, mine[j], k)

    def forward(seg, keys, values, p_ref, low, high, mask, first):
        size = keys.shape[0]
        small_t[:, :size] = values[...].T

        def visit(i, _):
            at = pl.ds(pl.multiple_of(i * tile, tile), tile)
            scores = dot_nt(keys[...], qrows[at, :])
            if mask is not None:
                scores = mask(scores)
            top = jnp.max(scores, axis=0, keepdims=True)
            powers = jnp.exp2((scores - top) * c)
            total = jnp.sum(powers, axis=0, keepdims=True)
            low_powers = powers.astype(BF16)
            p_ref[:, at] = low_powers
            weighted = dot(small_t[:, :size], low_powers)
            tops[seg : seg + 1, at] = top
            if first:
                acc[0:depth, at] = weighted
                acc[depth : depth + 1, at] = top
                acc[depth + 1 : depth + 2, at] = total
            else:
                before = acc[depth : depth + 1, at]
                fresh = jnp.maximum(before, top)
                old = jnp.exp2((before - fresh) * c)
                new = jnp.exp2((top - fresh) * c)
                acc[0:depth, at] = acc[0:depth, at] * old + weighted * new
                acc[depth : depth + 1, at] = fresh
                acc[depth + 1 : depth + 2, at] = acc[depth + 1 : depth + 2, at] * old + total * new
            return 0

        lax.fori_loop(low, high, visit, 0, unroll=True)

    def own_forward():
        for r in range(count):
            key_place = me_p * span + lax.broadcasted_iota(jnp.int32, (span, 1), 0)
            row_place = own[r][0] + lax.broadcasted_iota(jnp.int32, (1, tile), 1) % window

            def mask(scores):
                return jnp.where(key_place <= row_place, scores, NEG)

            forward(n_s, rk_ref.at[r], rv_ref.at[r], p_own, r * per, (r + 1) * per, mask, True)

    for name in ("offsets", "lengths", "q"):
        loads[name].wait()
    own = [(offsets[me_s * count + r], lengths[me_s * count + r]) for r in range(count)]
    line = lax.broadcasted_iota(jnp.int32, (window, 1), 0)
    for r in range(count):
        for h in range(group):
            at = pl.ds(r * height + h * window, window)
            head = pl.ds(h * depth, depth)
            qrows[at, :] = q_ref[r, :, head]
    loads["rk"].wait()
    loads["rv"].wait()
    own_forward()
    if relay:
        kv_copies[1, 0].wait_recv()
        send_kv(3, 0, kv.at[0, 0], 2)
        kv_copies[2, 1].wait_recv()
        send_kv(3, 1, kv.at[1, 1], 1)
    loads["g"].wait()
    for r in range(count):
        live = own[r][0] + line < own[r][1]
        for h in range(group):
            at = pl.ds(r * height + h * window, window)
            head = pl.ds(h * depth, depth)
            grows[at, :] = jnp.where(live, g_ref[r, :, head].astype(F32), 0.0).astype(BF16)
    for i in range(rows // tile):
        at = pl.ds(i * tile, tile)
        g_t[:, at] = grows[at, :].T

    loads["pk"].wait()
    loads["pv"].wait()
    forward(0, pk_ref, pv_ref, p_all.at[0], 0, count * per, None, False)
    acc_copies = []
    for k in range(1, n_s):
        for j in range(2):
            if not relay or (k, j) not in ((1, 0), (2, 1)):
                kv_copies[k, j].wait_recv()
        halves = count if k == n_s - 1 else 1
        for half in range(halves):
            low, high = half * count * per // halves, (half + 1) * count * per // halves
            forward(k, kv.at[k - 1, 0], kv.at[k - 1, 1], p_all.at[k], low, high, None, False)
            if k < n_s - 1:
                continue
            at = pl.ds(low * tile, (high - low) * tile)
            for to in range(1, n_p):
                copy = pltpu.make_async_remote_copy(
                    src_ref=acc.at[:, at],
                    dst_ref=acc_in.at[to - 1, :, at],
                    send_sem=acc_send.at[to - 1, half],
                    recv_sem=acc_recv.at[to - 1, half],
                    device_id={"prompt": (me_p + to) % n_p},
                    device_id_type=MESH,
                )
                copy.start()
                acc_copies.append((half, copy))

    for i in range(rows // tile):
        if i % per == 0:
            for half, copy in acc_copies:
                if half == i // per:
                    copy.wait_recv()
        at = pl.ds(i * tile, tile)
        top = acc[depth : depth + 1, at]
        for k in range(n_p - 1):
            top = jnp.maximum(top, acc_in[k, depth : depth + 1, at])
        decay = jnp.exp2((acc[depth : depth + 1, at] - top) * c)
        total = acc[depth + 1 : depth + 2, at] * decay
        weighted = acc[0:depth, at] * decay
        for k in range(n_p - 1):
            decay = jnp.exp2((acc_in[k, depth : depth + 1, at] - top) * c)
            total = total + acc_in[k, depth + 1 : depth + 2, at] * decay
            weighted = weighted + acc_in[k, 0:depth, at] * decay
        inverse = 1.0 / total
        output = weighted * inverse
        out_t[:, at] = output
        stats[0:1, at] = top
        stats[1:2, at] = inverse
        gq_t[:, at] = jnp.zeros((depth, tile), F32)
        r = i // per
        live = own[r][0] + line < own[r][1]
        by_row = output.T
        for part_h in range(tile // window):
            h = (i % per) * (tile // window) + part_h
            block = by_row[part_h * window : (part_h + 1) * window]
            att_ref[r, :, pl.ds(h * depth, depth)] = jnp.where(live, block, 0.0).astype(BF16)

    store(att_ref, att_hbm)

    def backward(seg, keys, values, p_ref, low, high):
        size = keys.shape[0]
        small_t[:, :size] = keys[...].T

        def visit(i, _):
            at = pl.ds(pl.multiple_of(i * tile, tile), tile)
            factor = jnp.exp2((tops[seg : seg + 1, at] - stats[0:1, at]) * c) * stats[1:2, at]
            grads = (g_t[:, at].astype(F32) * factor).astype(BF16)
            delta = jnp.sum(grads.astype(F32) * out_t[:, at], axis=0, keepdims=True)
            g_scaled[at, :] = grads.T
            weight_grad = dot(values[...], grads)
            score_grad = p_ref[:, at] * (weight_grad - delta).astype(BF16)
            ds[:size, at] = score_grad
            gq_t[:, at] += dot(small_t[:, :size], score_grad)
            return 0

        lax.fori_loop(low, high, visit, 0, unroll=True)
        span_rows = slice(low * tile, high * tile)
        value_grad = dot(p_ref[:, span_rows], g_scaled[span_rows, :])
        key_grad = dot(ds[:size, span_rows], qrows[span_rows, :]) * scale
        return key_grad, value_grad

    kvg_copies = []
    for k in range(n_s - 1, 0, -1):
        key_grad, value_grad = backward(
            k, kv.at[k - 1, 0], kv.at[k - 1, 1], p_all.at[k], 0, count * per
        )
        kvg_out[k - 1, 0] = key_grad.astype(BF16)
        kvg_out[k - 1, 1] = value_grad.astype(BF16)
        copy = pltpu.make_async_remote_copy(
            src_ref=kvg_out.at[k - 1],
            dst_ref=kvg_in.at[k - 1],
            send_sem=kvg_send.at[k - 1],
            recv_sem=kvg_recv.at[k - 1],
            device_id={"sample": from_sample(k)},
            device_id_type=MESH,
        )
        copy.start()
        kvg_copies.append(copy)
    key_grad, value_grad = backward(0, pk_ref, pv_ref, p_all.at[0], 0, count * per)
    kvg_own[0] = key_grad
    kvg_own[1] = value_grad
    for r in range(count):
        key_grad, value_grad = backward(
            n_s, rk_ref.at[r], rv_ref.at[r], p_own, r * per, (r + 1) * per
        )
        grk_ref[r] = key_grad.astype(BF16)
        grv_ref[r] = value_grad.astype(BF16)
        store(grk_ref.at[r], grk_hbm.at[r])
        store(grv_ref.at[r], grv_hbm.at[r])

    for i in range(rows // tile):
        at = pl.ds(i * tile, tile)
        r = i // per
        by_row = gq_t[:, at].T * scale
        for part_h in range(tile // window):
            h = (i % per) * (tile // window) + part_h
            for to in range(n_p):
                first = part_h * window + to * part
                gq_out[to, r, :, pl.ds(h * depth, depth)] = by_row[first : first + part]
    gq_copies = []
    for k in range(1, n_p):
        to = (me_p + k) % n_p
        copy = pltpu.make_async_remote_copy(
            src_ref=gq_out.at[to],
            dst_ref=gq_in.at[k - 1],
            send_sem=gq_send.at[k - 1],
            recv_sem=gq_recv.at[k - 1],
            device_id={"prompt": to},
            device_id_type=MESH,
        )
        copy.start()
        gq_copies.append(copy)
    for copy in kvg_copies:
        copy.wait_recv()
    for j, (ref, out) in enumerate(((gpk_ref, gpk_hbm), (gpv_ref, gpv_hbm))):
        total = kvg_own[j]
        for k in range(n_s - 1):
            total = total + kvg_in[k, j].astype(F32)
        ref[...] = total.astype(BF16)
        store(ref, out)
    for copy in gq_copies:
        copy.wait_recv()
    total = gq_out[me_p]
    for k in range(n_p - 1):
        total = total + gq_in[k]
    gq_ref[...] = total.astype(BF16)
    store(gq_ref, gq_hbm)
    for copy in stores:
        copy.wait()

    for copy in kv_copies.values():
        copy.wait_send()
    for copy in [copy for _, copy in acc_copies] + kvg_copies + gq_copies:
        copy.wait_send()


def write_out(*refs):
    sem = refs[-1]
    half = len(refs) // 2
    copies = [
        pltpu.make_async_copy(refs[i], refs[half + i], sem.at[i]) for i in range(half)
    ]
    for copy in copies:
        copy.start()
    for copy in copies:
        copy.wait()


def local(n_p, n_s, queries, prompt_keys, prompt_values, resp_keys, resp_values, cotangent, lengths, offsets):
    count, window, wide = queries.shape
    width, depth = prompt_keys.shape
    span = resp_keys.shape[1]
    rows = count * window * (wide // depth)
    tall = depth + 8
    hbm = pl.BlockSpec(memory_space=pltpu.HBM)
    shape = jax.ShapeDtypeStruct
    dma = pltpu.SemaphoreType.DMA
    peers = max(n_p - 1, 1)
    others = max(n_s - 1, 1)
    scratch = [
        pltpu.VMEM(queries.shape, BF16),
        pltpu.VMEM((count, window // n_p, wide), BF16),
        pltpu.VMEM(prompt_keys.shape, BF16),
        pltpu.VMEM(prompt_values.shape, BF16),
        pltpu.VMEM(resp_keys.shape, BF16),
        pltpu.VMEM(resp_values.shape, BF16),
        pltpu.SMEM(offsets.shape, offsets.dtype),
        pltpu.SMEM(lengths.shape, lengths.dtype),
        pltpu.VMEM(queries.shape, BF16),
        pltpu.VMEM(prompt_keys.shape, BF16),
        pltpu.VMEM(prompt_values.shape, BF16),
        pltpu.VMEM(resp_keys.shape, BF16),
        pltpu.VMEM(resp_values.shape, BF16),
        pltpu.VMEM(cotangent.shape, BF16),
        pltpu.VMEM((others, 2, width, depth), BF16),
        pltpu.VMEM((rows, depth), BF16),
        pltpu.VMEM((rows, depth), BF16),
        pltpu.VMEM((depth, rows), BF16),
        pltpu.VMEM((n_s, width, rows), BF16),
        pltpu.VMEM((span, rows), BF16),
        pltpu.VMEM((max(span, width), rows), BF16),
        pltpu.VMEM((rows, depth), BF16),
        pltpu.VMEM((depth, max(span, width)), BF16),
        pltpu.VMEM((tall, rows), F32),
        pltpu.VMEM((peers, tall, rows), F32),
        pltpu.VMEM((depth, rows), F32),
        pltpu.VMEM((-(-(n_s + 1) // 8) * 8, rows), F32),
        pltpu.VMEM((8, rows), F32),
        pltpu.VMEM((depth, rows), F32),
        pltpu.VMEM((2, width, depth), F32),
        pltpu.VMEM((others, 2, width, depth), BF16),
        pltpu.VMEM((others, 2, width, depth), BF16),
        pltpu.VMEM((n_p, count, window // n_p, wide), F32),
        pltpu.VMEM((peers, count, window // n_p, wide), F32),
        dma((others, 2)),
        dma((others, 2)),
        dma((peers, count)),
        dma((peers, count)),
        dma((others,)),
        dma((others,)),
        dma((peers,)),
        dma((peers,)),
        dma((8,)),
        dma((4 + 2 * count,)),
    ]
    results = pl.pallas_call(
        functools.partial(kernel, n_p, n_s),
        out_shape=(
            shape(queries.shape, BF16),
            shape((count, window // n_p, wide), BF16),
            shape(prompt_keys.shape, BF16),
            shape(prompt_values.shape, BF16),
            shape(resp_keys.shape, BF16),
            shape(resp_values.shape, BF16),
        ),
        in_specs=[hbm] * 8,
        out_specs=[hbm] * 6,
        scratch_shapes=scratch,
        compiler_params=pltpu.CompilerParams(
            collective_id=0, has_side_effects=True, vmem_limit_bytes=62 * 1024 * 1024
        ),
    )(offsets, lengths, queries, prompt_keys, prompt_values, resp_keys, resp_values, cotangent)
    return pl.pallas_call(
        write_out,
        out_shape=tuple(shape(result.shape, result.dtype) for result in results),
        in_specs=[hbm] * len(results),
        out_specs=[hbm] * len(results),
        scratch_shapes=[dma((len(results),))],
        compiler_params=pltpu.CompilerParams(vmem_limit_bytes=62 * 1024 * 1024),
    )(*results)


def solution(mesh):
    return jax.shard_map(
        functools.partial(local, mesh.shape["prompt"], mesh.shape["sample"]),
        mesh=mesh,
        in_specs=(
            P("sample", None, "head"),
            P(("prompt", "sample"), "head"),
            P(("prompt", "sample"), "head"),
            P("sample", "prompt", "head"),
            P("sample", "prompt", "head"),
            P("sample", None, "head"),
            P(),
            P(),
        ),
        out_specs=(
            P("sample", None, "head"),
            P("sample", "prompt", "head"),
            P(("prompt", "sample"), "head"),
            P(("prompt", "sample"), "head"),
            P("sample", "prompt", "head"),
            P("sample", "prompt", "head"),
        ),
        check_vma=False,
    )
```

```python
import functools
import math

import jax
import jax.numpy as jnp
from jax import lax
from jax.experimental import pallas as pl
from jax.experimental.pallas import tpu as pltpu
from jax.sharding import PartitionSpec as P

NEG = -1e30
MESH = pl.DeviceIdType.MESH
F32 = jnp.float32
BF16 = jnp.bfloat16


def dot(a, b):
    return jnp.dot(a, b, preferred_element_type=F32)


def dot_nt(a, b):
    return lax.dot_general(a, b, (((1,), (1,)), ((), ())), preferred_element_type=F32)


def kernel(
    n_p,
    n_s,
    offsets_hbm,
    lengths_hbm,
    q_hbm,
    pk_hbm,
    pv_hbm,
    rk_hbm,
    rv_hbm,
    g_hbm,
    att_hbm,
    gq_hbm,
    gpk_hbm,
    gpv_hbm,
    grk_hbm,
    grv_hbm,
    att_ref,
    gq_ref,
    gpk_ref,
    gpv_ref,
    grk_ref,
    grv_ref,
    offsets,
    lengths,
    q_ref,
    pk_ref,
    pv_ref,
    rk_ref,
    rv_ref,
    g_ref,
    kv,
    qrows,
    grows,
    g_t,
    p_all,
    p_own,
    ds,
    g_scaled,
    small_t,
    acc,
    acc_in,
    out_t,
    tops,
    stats,
    gq_t,
    kvg_own,
    kvg_out,
    kvg_in,
    gq_out,
    gq_in,
    kv_send,
    kv_recv,
    acc_send,
    acc_recv,
    kvg_send,
    kvg_recv,
    gq_send,
    gq_recv,
    load_sem,
    store_sem,
):
    count, window, wide = q_ref.shape
    width, depth = pk_ref.shape
    span = rk_ref.shape[1]
    group = wide // depth
    height = window * group
    rows = count * height
    tile = math.gcd(height, 512)
    per = height // tile
    scale = 1.0 / math.sqrt(depth)
    c = scale * math.log2(math.e)
    me_s = lax.axis_index("sample")
    me_p = lax.axis_index("prompt")
    part = window // n_p

    def to_sample(k):
        if n_s == 4:
            return ((me_s // 2 + k // 2) % 2) * 2 + (me_s % 2 + k % 2) % 2
        return (me_s + k) % n_s

    def from_sample(k):
        if n_s == 4:
            return to_sample(k)
        return (me_s + n_s - k) % n_s

    loads = {}
    for name, src, dst in (
        ("offsets", offsets_hbm, offsets),
        ("lengths", lengths_hbm, lengths),
        ("q", q_hbm, q_ref),
        ("rk", rk_hbm, rk_ref),
        ("rv", rv_hbm, rv_ref),
        ("pk", pk_hbm, pk_ref),
        ("pv", pv_hbm, pv_ref),
        ("g", g_hbm, g_ref),
    ):
        loads[name] = pltpu.make_async_copy(src, dst, load_sem.at[len(loads)])
        loads[name].start()

    barrier = pltpu.get_barrier_semaphore()
    for k in range(1, n_s):
        pl.semaphore_signal(barrier, inc=1, device_id={"sample": to_sample(k)}, device_id_type=MESH)
    for k in range(1, n_p):
        pl.semaphore_signal(
            barrier, inc=1, device_id={"prompt": (me_p + k) % n_p}, device_id_type=MESH
        )
    pl.semaphore_wait(barrier, n_s - 1 + n_p - 1)

    stores = []

    def store(src, dst):
        stores.append(pltpu.make_async_copy(src, dst, store_sem.at[len(stores)]))
        stores[-1].start()

    kv_copies = {}

    def send_kv(k, j, src, to):
        copy = pltpu.make_async_remote_copy(
            src_ref=src,
            dst_ref=kv.at[k - 1, j],
            send_sem=kv_send.at[k - 1, j],
            recv_sem=kv_recv.at[k - 1, j],
            device_id={"sample": to_sample(to)},
            device_id_type=MESH,
        )
        copy.start()
        kv_copies[k, j] = copy

    relay = n_s == 4
    mine = (pk_hbm, pv_hbm)
    if relay:
        for k, j in ((1, 0), (2, 1), (1, 1), (2, 0)):
            send_kv(k, j, mine[j], k)
    else:
        for k in range(1, n_s):
            for j in range(2):
                send_kv(k, j, mine[j], k)

    def forward(seg, keys, values, p_ref, low, high, mask, first):
        size = keys.shape[0]
        small_t[:, :size] = values[...].T

        def visit(i, _):
            at = pl.ds(pl.multiple_of(i * tile, tile), tile)
            scores = dot_nt(keys[...], qrows[at, :])
            if mask is not None:
                scores = mask(scores)
            top = jnp.max(scores, axis=0, keepdims=True)
            powers = jnp.exp2((scores - top) * c)
            total = jnp.sum(powers, axis=0, keepdims=True)
            low_powers = powers.astype(BF16)
            p_ref[:, at] = low_powers
            weighted = dot(small_t[:, :size], low_powers)
            tops[seg : seg + 1, at] = top
            if first:
                acc[0:depth, at] = weighted
                acc[depth : depth + 1, at] = top
                acc[depth + 1 : depth + 2, at] = total
            else:
                before = acc[depth : depth + 1, at]
                fresh = jnp.maximum(before, top)
                old = jnp.exp2((before - fresh) * c)
                new = jnp.exp2((top - fresh) * c)
                acc[0:depth, at] = acc[0:depth, at] * old + weighted * new
                acc[depth : depth + 1, at] = fresh
                acc[depth + 1 : depth + 2, at] = acc[depth + 1 : depth + 2, at] * old + total * new
            return 0

        lax.fori_loop(low, high, visit, 0, unroll=True)

    def own_forward():
        for r in range(count):
            key_place = me_p * span + lax.broadcasted_iota(jnp.int32, (span, 1), 0)
            row_place = own[r][0] + lax.broadcasted_iota(jnp.int32, (1, tile), 1) % window

            def mask(scores):
                return jnp.where(key_place <= row_place, scores, NEG)

            forward(n_s, rk_ref.at[r], rv_ref.at[r], p_own, r * per, (r + 1) * per, mask, True)

    for name in ("offsets", "lengths", "q"):
        loads[name].wait()
    own = [(offsets[me_s * count + r], lengths[me_s * count + r]) for r in range(count)]
    line = lax.broadcasted_iota(jnp.int32, (window, 1), 0)
    for r in range(count):
        for h in range(group):
            at = pl.ds(r * height + h * window, window)
            head = pl.ds(h * depth, depth)
            qrows[at, :] = q_ref[r, :, head]
    loads["rk"].wait()
    loads["rv"].wait()
    own_forward()
    if relay:
        kv_copies[1, 0].wait_recv()
        send_kv(3, 0, kv.at[0, 0], 2)
        kv_copies[2, 1].wait_recv()
        send_kv(3, 1, kv.at[1, 1], 1)
    loads["g"].wait()
    for r in range(count):
        live = own[r][0] + line < own[r][1]
        for h in range(group):
            at = pl.ds(r * height + h * window, window)
            head = pl.ds(h * depth, depth)
            grows[at, :] = jnp.where(live, g_ref[r, :, head].astype(F32), 0.0).astype(BF16)
    for i in range(rows // tile):
        at = pl.ds(i * tile, tile)
        g_t[:, at] = grows[at, :].T

    loads["pk"].wait()
    loads["pv"].wait()
    forward(0, pk_ref, pv_ref, p_all.at[0], 0, count * per, None, False)
    acc_copies = []
    for k in range(1, n_s):
        for j in range(2):
            if not relay or (k, j) not in ((1, 0), (2, 1)):
                kv_copies[k, j].wait_recv()
        halves = count if k == n_s - 1 else 1
        for half in range(halves):
            low, high = half * count * per // halves, (half + 1) * count * per // halves
            forward(k, kv.at[k - 1, 0], kv.at[k - 1, 1], p_all.at[k], low, high, None, False)
            if k < n_s - 1:
                continue
            at = pl.ds(low * tile, (high - low) * tile)
            for to in range(1, n_p):
                copy = pltpu.make_async_remote_copy(
                    src_ref=acc.at[:, at],
                    dst_ref=acc_in.at[to - 1, :, at],
                    send_sem=acc_send.at[to - 1, half],
                    recv_sem=acc_recv.at[to - 1, half],
                    device_id={"prompt": (me_p + to) % n_p},
                    device_id_type=MESH,
                )
                copy.start()
                acc_copies.append((half, copy))

    for i in range(rows // tile):
        if i % per == 0:
            for half, copy in acc_copies:
                if half == i // per:
                    copy.wait_recv()
        at = pl.ds(i * tile, tile)
        top = acc[depth : depth + 1, at]
        for k in range(n_p - 1):
            top = jnp.maximum(top, acc_in[k, depth : depth + 1, at])
        decay = jnp.exp2((acc[depth : depth + 1, at] - top) * c)
        total = acc[depth + 1 : depth + 2, at] * decay
        weighted = acc[0:depth, at] * decay
        for k in range(n_p - 1):
            decay = jnp.exp2((acc_in[k, depth : depth + 1, at] - top) * c)
            total = total + acc_in[k, depth + 1 : depth + 2, at] * decay
            weighted = weighted + acc_in[k, 0:depth, at] * decay
        inverse = 1.0 / total
        output = weighted * inverse
        out_t[:, at] = output
        stats[0:1, at] = top
        stats[1:2, at] = inverse
        gq_t[:, at] = jnp.zeros((depth, tile), F32)
        r = i // per
        live = own[r][0] + line < own[r][1]
        by_row = output.T
        for part_h in range(tile // window):
            h = (i % per) * (tile // window) + part_h
            block = by_row[part_h * window : (part_h + 1) * window]
            att_ref[r, :, pl.ds(h * depth, depth)] = jnp.where(live, block, 0.0).astype(BF16)

    store(att_ref, att_hbm)

    def backward(seg, keys, values, p_ref, low, high):
        size = keys.shape[0]
        small_t[:, :size] = keys[...].T

        def visit(i, _):
            at = pl.ds(pl.multiple_of(i * tile, tile), tile)
            factor = jnp.exp2((tops[seg : seg + 1, at] - stats[0:1, at]) * c) * stats[1:2, at]
            grads = (g_t[:, at].astype(F32) * factor).astype(BF16)
            delta = jnp.sum(grads.astype(F32) * out_t[:, at], axis=0, keepdims=True)
            g_scaled[at, :] = grads.T
            weight_grad = dot(values[...], grads)
            score_grad = p_ref[:, at] * (weight_grad - delta).astype(BF16)
            ds[:size, at] = score_grad
            gq_t[:, at] += dot(small_t[:, :size], score_grad)
            return 0

        lax.fori_loop(low, high, visit, 0, unroll=True)
        span_rows = slice(low * tile, high * tile)
        value_grad = dot(p_ref[:, span_rows], g_scaled[span_rows, :])
        key_grad = dot(ds[:size, span_rows], qrows[span_rows, :]) * scale
        return key_grad, value_grad

    kvg_copies = []
    for k in range(n_s - 1, 0, -1):
        key_grad, value_grad = backward(
            k, kv.at[k - 1, 0], kv.at[k - 1, 1], p_all.at[k], 0, count * per
        )
        kvg_out[k - 1, 0] = key_grad.astype(BF16)
        kvg_out[k - 1, 1] = value_grad.astype(BF16)
        copy = pltpu.make_async_remote_copy(
            src_ref=kvg_out.at[k - 1],
            dst_ref=kvg_in.at[k - 1],
            send_sem=kvg_send.at[k - 1],
            recv_sem=kvg_recv.at[k - 1],
            device_id={"sample": from_sample(k)},
            device_id_type=MESH,
        )
        copy.start()
        kvg_copies.append(copy)
    key_grad, value_grad = backward(0, pk_ref, pv_ref, p_all.at[0], 0, count * per)
    kvg_own[0] = key_grad
    kvg_own[1] = value_grad
    for r in range(count):
        key_grad, value_grad = backward(
            n_s, rk_ref.at[r], rv_ref.at[r], p_own, r * per, (r + 1) * per
        )
        grk_ref[r] = key_grad.astype(BF16)
        grv_ref[r] = value_grad.astype(BF16)
        store(grk_ref.at[r], grk_hbm.at[r])
        store(grv_ref.at[r], grv_hbm.at[r])

    for i in range(rows // tile):
        at = pl.ds(i * tile, tile)
        r = i // per
        by_row = gq_t[:, at].T * scale
        for part_h in range(tile // window):
            h = (i % per) * (tile // window) + part_h
            for to in range(n_p):
                first = part_h * window + to * part
                gq_out[to, r, :, pl.ds(h * depth, depth)] = by_row[first : first + part]
    gq_copies = []
    for k in range(1, n_p):
        to = (me_p + k) % n_p
        copy = pltpu.make_async_remote_copy(
            src_ref=gq_out.at[to],
            dst_ref=gq_in.at[k - 1],
            send_sem=gq_send.at[k - 1],
            recv_sem=gq_recv.at[k - 1],
            device_id={"prompt": to},
            device_id_type=MESH,
        )
        copy.start()
        gq_copies.append(copy)
    for copy in kvg_copies:
        copy.wait_recv()
    for j, (ref, out) in enumerate(((gpk_ref, gpk_hbm), (gpv_ref, gpv_hbm))):
        total = kvg_own[j]
        for k in range(n_s - 1):
            total = total + kvg_in[k, j].astype(F32)
        ref[...] = total.astype(BF16)
        store(ref, out)
    for copy in gq_copies:
        copy.wait_recv()
    total = gq_out[me_p]
    for k in range(n_p - 1):
        total = total + gq_in[k]
    gq_ref[...] = total.astype(BF16)
    store(gq_ref, gq_hbm)
    for copy in stores:
        copy.wait()

    for copy in kv_copies.values():
        copy.wait_send()
    for copy in [copy for _, copy in acc_copies] + kvg_copies + gq_copies:
        copy.wait_send()


def write_out(count, *refs):
    sources, targets, held = refs[:count], refs[count : 2 * count], refs[2 * count : 3 * count]
    load_sem, store_sem = refs[3 * count :]
    loads = [pltpu.make_async_copy(sources[i], held[i], load_sem.at[i]) for i in range(count)]
    stores = [pltpu.make_async_copy(held[i], targets[i], store_sem.at[i]) for i in range(count)]
    for copy in loads:
        copy.start()
    for load, store in zip(loads, stores):
        load.wait()
        store.start()
    for copy in stores:
        copy.wait()


def local(n_p, n_s, queries, prompt_keys, prompt_values, resp_keys, resp_values, cotangent, lengths, offsets):
    count, window, wide = queries.shape
    width, depth = prompt_keys.shape
    span = resp_keys.shape[1]
    rows = count * window * (wide // depth)
    tall = depth + 8
    hbm = pl.BlockSpec(memory_space=pltpu.HBM)
    shape = jax.ShapeDtypeStruct
    dma = pltpu.SemaphoreType.DMA
    peers = max(n_p - 1, 1)
    others = max(n_s - 1, 1)
    scratch = [
        pltpu.VMEM(queries.shape, BF16),
        pltpu.VMEM((count, window // n_p, wide), BF16),
        pltpu.VMEM(prompt_keys.shape, BF16),
        pltpu.VMEM(prompt_values.shape, BF16),
        pltpu.VMEM(resp_keys.shape, BF16),
        pltpu.VMEM(resp_values.shape, BF16),
        pltpu.SMEM(offsets.shape, offsets.dtype),
        pltpu.SMEM(lengths.shape, lengths.dtype),
        pltpu.VMEM(queries.shape, BF16),
        pltpu.VMEM(prompt_keys.shape, BF16),
        pltpu.VMEM(prompt_values.shape, BF16),
        pltpu.VMEM(resp_keys.shape, BF16),
        pltpu.VMEM(resp_values.shape, BF16),
        pltpu.VMEM(cotangent.shape, BF16),
        pltpu.VMEM((others, 2, width, depth), BF16),
        pltpu.VMEM((rows, depth), BF16),
        pltpu.VMEM((rows, depth), BF16),
        pltpu.VMEM((depth, rows), BF16),
        pltpu.VMEM((n_s, width, rows), BF16),
        pltpu.VMEM((span, rows), BF16),
        pltpu.VMEM((max(span, width), rows), BF16),
        pltpu.VMEM((rows, depth), BF16),
        pltpu.VMEM((depth, max(span, width)), BF16),
        pltpu.VMEM((tall, rows), F32),
        pltpu.VMEM((peers, tall, rows), F32),
        pltpu.VMEM((depth, rows), F32),
        pltpu.VMEM((-(-(n_s + 1) // 8) * 8, rows), F32),
        pltpu.VMEM((8, rows), F32),
        pltpu.VMEM((depth, rows), F32),
        pltpu.VMEM((2, width, depth), F32),
        pltpu.VMEM((others, 2, width, depth), BF16),
        pltpu.VMEM((others, 2, width, depth), BF16),
        pltpu.VMEM((n_p, count, window // n_p, wide), F32),
        pltpu.VMEM((peers, count, window // n_p, wide), F32),
        dma((others, 2)),
        dma((others, 2)),
        dma((peers, count)),
        dma((peers, count)),
        dma((others,)),
        dma((others,)),
        dma((peers,)),
        dma((peers,)),
        dma((8,)),
        dma((4 + 2 * count,)),
    ]
    results = pl.pallas_call(
        functools.partial(kernel, n_p, n_s),
        out_shape=(
            shape(queries.shape, BF16),
            shape((count, window // n_p, wide), BF16),
            shape(prompt_keys.shape, BF16),
            shape(prompt_values.shape, BF16),
            shape(resp_keys.shape, BF16),
            shape(resp_values.shape, BF16),
        ),
        in_specs=[hbm] * 8,
        out_specs=[hbm] * 6,
        scratch_shapes=scratch,
        compiler_params=pltpu.CompilerParams(
            collective_id=0, has_side_effects=True, vmem_limit_bytes=62 * 1024 * 1024
        ),
    )(offsets, lengths, queries, prompt_keys, prompt_values, resp_keys, resp_values, cotangent)
    return pl.pallas_call(
        functools.partial(write_out, len(results)),
        out_shape=tuple(shape(result.shape, result.dtype) for result in results),
        in_specs=[hbm] * len(results),
        out_specs=[hbm] * len(results),
        scratch_shapes=[pltpu.VMEM(result.shape, result.dtype) for result in results]
        + [dma((len(results),))] * 2,
        compiler_params=pltpu.CompilerParams(vmem_limit_bytes=62 * 1024 * 1024),
    )(*results)


def solution(mesh):
    return jax.shard_map(
        functools.partial(local, mesh.shape["prompt"], mesh.shape["sample"]),
        mesh=mesh,
        in_specs=(
            P("sample", None, "head"),
            P(("prompt", "sample"), "head"),
            P(("prompt", "sample"), "head"),
            P("sample", "prompt", "head"),
            P("sample", "prompt", "head"),
            P("sample", None, "head"),
            P(),
            P(),
        ),
        out_specs=(
            P("sample", None, "head"),
            P("sample", "prompt", "head"),
            P(("prompt", "sample"), "head"),
            P(("prompt", "sample"), "head"),
            P("sample", "prompt", "head"),
            P("sample", "prompt", "head"),
        ),
        check_vma=False,
    )
```
